512 devices in a mesh: fsdp: 8 (over y, core), expert: 64 (over z, x).
Axes of the slice: x: 4, y: 4, z: 16, core: 2. Of those that a mesh axis runs over, the one named last changes fastest.
Arguments:
- resid: bfloat16 [64, 64, 4096], P('expert', None, 'fsdp'), may hold values from -200 to 200
- norm_gain: float32 [4096], P('fsdp'), may hold values from 0.1 to 1.9
- lengths: int32 [64], replicated, may hold values from 1 to 64, 3072 in all
- route_ids: int32 [64, 64, 2], P('expert'), may hold values from 0 to 7, all different within a row; in each aligned block of 64 rows (0 to 63, 64 to 127, ..., all dimensions but the last counted through in order) at most 24 rows name the same one
- route_weight: float32 [64, 64, 2], P('expert'), may hold values from 0.2 to 1
- w_gate: bfloat16 [4096, 98304], P('fsdp', 'expert'), may hold values from -0.09375 to 0.09375
- w_up: bfloat16 [4096, 98304], P('fsdp', 'expert'), may hold values from -0.09375 to 0.09375
- w_down: bfloat16 [98304, 4096], P('expert', 'fsdp'), may hold values from -0.0546875 to 0.0546875
Outputs:
- moe_out: bfloat16 [64, 64, 4096], P('expert', None, 'fsdp')
The draws below stay inside these ranges and needn't reach their ends.
Inputs may be any that keep to these rules, and one draw needn't show every extreme that they name: `route_ids`: each row names 2 different experts; within one prompt no expert is named by more than 24 rows.
All inputs are finite; a program needn't handle non-finite values.
Results may differ from the reference program's by a relative error of at most 0.029.
Values may be sent and summed in bfloat16 or wider, within the bound.
A program may use at most 64 MiB of HBM per device.

```python
import math
import jax
import jax.numpy as jnp
import numpy as np
from jax import lax

D = 4096
EXPERTS = 8
TOP = 2
FF_DEV = 1536
LEN = 64
CAP = 24
PROMPTS = 64
FFW = 12288
N_FSDP = 8
N_EXPERT = 64


def draw_resid(key, part):
    key = jax.random.fold_in(key, 17)
    key_noise, key_col, key_row = jax.random.split(key, 3)
    shape = (PROMPTS, LEN, D)
    ramp = jnp.arange(D, dtype=jnp.float32) / D
    col_scale = jnp.exp(jnp.log(3.0) * ramp + jnp.log(10.0) * (jax.random.uniform(key_col, (D,), jnp.float32) - 0.5))
    row_scale = jnp.exp(jnp.log(10.0) * (jax.random.uniform(key_row, (PROMPTS, LEN, 1), jnp.float32) - 0.5))
    noise = jnp.clip(jax.random.normal(key_noise, shape, jnp.float32), -6.0, 6.0)
    return (noise * row_scale * col_scale).astype(jnp.bfloat16)


def levels(key, dims, shards, low, high):
    loudness = 1.0
    for position, blocks in shards:
        heights = jax.random.uniform(jax.random.fold_in(jax.random.fold_in(key, 6), position), (blocks,), jnp.float32, low / len(shards), high / len(shards))
        loudness = loudness * jnp.repeat(jnp.exp(heights), dims[position] // blocks).reshape((-1,) + (1,) * (len(dims) - 1 - position))
    return loudness


def split_up(number_of, total, bound, lean):
    weights = [(1 << 20) // math.isqrt(rank ** lean) + 1 for rank in range(2, number_of + 1)]
    rest, holding = total - bound - (number_of - 1), [1] * (number_of - 1)
    while rest > 0:
        movable = [i for i in range(number_of - 1) if holding[i] < bound]
        mass, remaining = sum([weights[i] for i in movable]), rest
        for i in movable:
            addition = min(bound - holding[i], max(1, remaining * weights[i] // mass), rest)
            holding[i] = holding[i] + addition
            rest = rest - addition
    return np.array([bound] + holding)


def uneven_parts(rng, count, total, bound, lean):
    if count == 2:
        one = jax.random.randint(rng, (), max(1, total - bound), min(bound, total - 1) + 1)
        return jnp.stack([one, total - one])
    sizes = jnp.asarray(split_up(count, total, bound, lean), jnp.int32)
    twos = (count - 1) // 2
    source_of, taker = sizes[1:1 + 2 * twos:2], sizes[2:2 + 2 * twos:2]
    room = jnp.minimum(source_of - 1, bound - taker)
    moved = jax.random.randint(jax.random.fold_in(rng, 1), (twos,), 0, 1 << 20) % (room + 1)
    sizes = sizes.at[1:1 + 2 * twos:2].set(source_of - moved).at[2:2 + 2 * twos:2].set(taker + moved)
    return sizes[jax.random.permutation(jax.random.fold_in(rng, 2), count)]


def deal_out(rng, own, number, rows, count, top, bound, lean):
    sequence = jax.random.permutation(rng, count)
    crowded, usual = shares(count, rows * top, bound, lean, True), shares(count, rows * top, bound, lean, False)
    places = jnp.arange(count)

    def named(sizes, offset_by):
        used = int((sizes > 0).sum())
        fixed = max(1, used // 4)
        shifted = fixed + (places - fixed + offset_by * (used - fixed)) % max(1, count - fixed)
        return jnp.zeros((count,), jnp.int32).at[sequence[jnp.where(places < fixed, places, shifted)]].set(jnp.asarray(sizes, jnp.int32))

    sizes = jnp.where(number % 4 == 0, named(crowded, number // 4), named(usual, number - number // 4 - 1))
    mixed = jax.random.permutation(jax.random.fold_in(own, 3), count)
    donor, taker = mixed[0:count // 2 * 2:2], mixed[1:count // 2 * 2:2]
    room = jnp.minimum(sizes[donor] - 1, bound - sizes[taker]) // 2
    room = jnp.where((donor == sequence[0]) | (taker == sequence[0]) | (sizes[taker] == 0), 0, jnp.maximum(room, 0))
    shifted = jax.random.randint(jax.random.fold_in(own, 4), (count // 2,), 0, 1 << 20) % (room + 1)
    sizes = sizes.at[donor].add(-shifted).at[taker].add(shifted)
    items = jnp.searchsorted(jnp.cumsum(sizes), jnp.arange(rows * top), side="right").astype(jnp.int32)
    grid = items.reshape(top, rows).T
    grid = grid[jax.random.permutation(jax.random.fold_in(own, 1), rows)]
    offset_by = jax.random.randint(jax.random.fold_in(own, 2), (rows, 1), 0, top)
    return jnp.take_along_axis(grid, (jnp.arange(top)[None, :] + offset_by) % top, axis=1)


def shares(amount, total, reach, slope, full):
    loads = [(1 << 20) // math.isqrt(standing ** slope) + 1 for standing in range(1, amount + 1)]
    largest = reach if full else min(reach, max(-(-total // amount), total * loads[0] // sum(loads)))
    least = 1 if total - largest >= amount - 1 else 0
    counts, rest = [largest] + [least] * (amount - 1), total - largest - least * (amount - 1)
    while rest > 0:
        free = [i for i in range(1, amount) if counts[i] < largest] or [i for i in range(1, amount) if counts[i] < reach]
        whole, left = sum([loads[i] for i in free]), rest
        for i in free:
            more = min(reach - counts[i], max(1, left * loads[i] // whole), rest)
            counts[i] = counts[i] + more
            rest = rest - more
    return np.array(counts)


def normal_values(stream_key, extent, scale, bound, cuts=(), kind=jnp.bfloat16):
    values = scale * jax.random.normal(stream_key, extent, jnp.float32)
    if cuts:
        values = values * levels(stream_key, extent, cuts, -0.22, 0.18)
    return jnp.clip(values, -bound, bound).astype(kind)


def setup_inputs(seed: int = 0) -> dict:
    seeds = jax.random.split(jax.random.key(seed), 9)
    resid = draw_resid(jax.random.fold_in(seeds[8], 71), 0)
    norm_gain = jnp.clip(1.0 + 0.18 * jax.random.normal(seeds[1], (D,), jnp.float32), 0.1, 1.9)
    lengths = uneven_parts(seeds[2], PROMPTS, PROMPTS * LEN * 3 // 4, LEN, 2).astype(jnp.int32)
    route_ids_keys = jax.random.split(jax.random.fold_in(seeds[3], 1), PROMPTS * LEN // LEN)
    route_ids_turns = jax.random.permutation(jax.random.fold_in(seeds[3], 3), PROMPTS * LEN // LEN)
    route_ids = jax.vmap(lambda own, number: deal_out(jax.random.fold_in(seeds[3], 2), own, number, LEN, EXPERTS, TOP, CAP, 2))(route_ids_keys, route_ids_turns).reshape((PROMPTS, LEN, TOP))
    route_weight = jnp.clip(0.2 + 0.8 * jax.random.uniform(seeds[4], (PROMPTS, LEN, TOP), jnp.float32) ** levels(seeds[4], (PROMPTS, LEN, TOP), ((0, 64),), -0.2, 0.2), 0.2, 1.0)
    w_gate = normal_values(seeds[5], (D, EXPERTS * FFW), D ** -0.5, 0.09375, ((0, 8), (1, 64)))
    w_up = normal_values(seeds[6], (D, EXPERTS * FFW), D ** -0.5, 0.09375, ((0, 8), (1, 64)))
    w_down = normal_values(seeds[7], (EXPERTS * FFW, D), FFW ** -0.5, 0.0546875, ((0, 64), (1, 8)))
    return {"resid": resid, "norm_gain": norm_gain, "lengths": lengths, "route_ids": route_ids, "route_weight": route_weight, "w_gate": w_gate, "w_up": w_up, "w_down": w_down}


def block_sum(blocks, weight):
    panels = weight.astype(jnp.float32).reshape(N_FSDP, D // N_FSDP, weight.shape[1])
    partial_value = jnp.einsum('rfd,fdk->rfk', blocks, panels, precision=lax.Precision.HIGHEST)
    rounded = lax.optimization_barrier(partial_value.astype(jnp.bfloat16))
    return lax.optimization_barrier(jnp.sum(rounded.astype(jnp.float32), axis=1))

def reference(resid, norm_gain, lengths, route_ids, route_weight, w_gate, w_up, w_down):
    prompts, length = (resid.shape[0], resid.shape[1])
    live_rows = (jnp.arange(length, dtype=jnp.int32)[None, :] < lengths[:, None]).astype(jnp.float32)
    resid_rows = resid.astype(jnp.float32)
    square = lax.optimization_barrier(jnp.mean(resid_rows * resid_rows, axis=-1, keepdims=True))
    normed = (resid_rows * lax.rsqrt(square + 1e-05) * norm_gain).astype(jnp.bfloat16)
    rows_in = normed.astype(jnp.float32)
    group_size = N_EXPERT // EXPERTS
    feat_share = D // N_FSDP
    slot_iota = jnp.arange(CAP, dtype=jnp.int32)

    def one_expert(combined, expert_id):
        hit_rows = jnp.any(route_ids == expert_id, axis=-1).astype(jnp.int32)
        slot_rank = jnp.cumsum(hit_rows, axis=1) - 1
        select = ((hit_rows[:, None, :] == 1) & (slot_rank[:, None, :] == slot_iota[None, :, None])).astype(jnp.float32)
        slot_rows = jnp.einsum('pct,ptd->pcd', select, rows_in, precision=lax.Precision.HIGHEST)
        blocks = slot_rows.reshape(prompts * CAP, N_FSDP, feat_share)
        result = jnp.zeros((prompts * CAP, D), jnp.float32)
        for slice_id in range(group_size):
            col_start = ((expert_id * group_size + slice_id) * FF_DEV).astype(jnp.int32)
            gate_sum = block_sum(blocks, lax.dynamic_slice_in_dim(w_gate, col_start, FF_DEV, 1))
            up_sum = block_sum(blocks, lax.dynamic_slice_in_dim(w_up, col_start, FF_DEV, 1))
            hidden = (jax.nn.silu(gate_sum) * up_sum).astype(jnp.bfloat16)
            out_part = jnp.dot(hidden, lax.dynamic_slice_in_dim(w_down, col_start, FF_DEV, 0), preferred_element_type=jnp.float32).astype(jnp.bfloat16)
            result = result + out_part.astype(jnp.float32)
        gate_mix = lax.optimization_barrier(jnp.sum(route_weight * (route_ids == expert_id).astype(jnp.float32), axis=-1))
        placed = jnp.einsum('pct,pcd->ptd', select, result.reshape(prompts, CAP, D), precision=lax.Precision.HIGHEST)
        return (combined + gate_mix[:, :, None] * placed, None)
    combined, _ = lax.scan(one_expert, jnp.zeros((prompts, length, D), jnp.float32), jnp.arange(EXPERTS, dtype=jnp.int32))
    return (live_rows[:, :, None] * combined).astype(jnp.bfloat16)
```

```python
import jax
import jax.numpy as jnp
from jax import lax
from jax.experimental import pallas as pl
from jax.experimental.pallas import tpu as pltpu
from jax.sharding import PartitionSpec as P

MESH = pl.DeviceIdType.MESH
D = 4096
EXPERTS = 8
CAP = 24
LEN = 64
FEAT = 512
HALF = 768
BLOCK = 2 * CAP
WIDE = 256
CHUNKS = 8
ROWS = 8 * CAP
OWN = ROWS // 4
ORDER = (0, 2, 6, 3, 5, 4, 1, 7)
F32 = jnp.float32
BF16 = jnp.bfloat16


def order_of(i):
    distance = ORDER[0] + 0 * i
    for k in range(1, CHUNKS):
        distance = distance + (ORDER[k] - ORDER[k - 1]) * ((i + CHUNKS - k) // CHUNKS)
    return distance


def to_blocks(left, right):
    return jnp.concatenate([left.reshape(8, CAP, WIDE), right.reshape(8, CAP, WIDE)], axis=1)


def from_blocks(blocks):
    return blocks[:, :CAP, :].reshape(ROWS, WIDE), blocks[:, CAP:, :].reshape(ROWS, WIDE)


def kernel(lengths, resid, gain, chosen, weight, w_gate, w_up, w_down, out,
           squares, sent, slots, w_in, w_out, part, ra, rb, hid, out_mine, out_sent, out_got,
           xs, xr, ret_sent, ret,
           sq_s, sq_r, w_l, w_s, w_r, a_s, a_r, c_s, c_r, d_s, d_r, e_s, e_r, f_s, f_r, g_s, g_r,
           h_s, h_r, i_s, i_r, j_s, j_r, l_s, l_r):
    f = lax.axis_index("fsdp")
    p = lax.axis_index("expert")
    y, core = f // 2, f % 2
    z, x = p // 4, p % 4
    expert, par = z // 2, z % 2
    member = par * 4 + x
    right, left, opp = (y + 1) % 4, (y + 3) % 4, (y + 2) % 4

    def same_group(j):
        other = (member + j) % 8
        return (f, (2 * expert + other // 4) * 4 + other % 4)

    def along_z(e):
        return (f, (2 * e + par) * 4 + x)

    def at_y(row):
        return (row * 2 + core, p)

    twin = (y * 2 + 1 - core, p)

    def expert_of(i):
        return (expert + CHUNKS - order_of(i)) % CHUNKS

    def source_of(i):
        return (expert + order_of(i)) % CHUNKS

    def remote(src, dst, send, recv, device):
        return pltpu.make_async_remote_copy(
            src_ref=src, dst_ref=dst, send_sem=send, recv_sem=recv, device_id=device, device_id_type=MESH
        )

    def cp_sq(j):
        return remote(squares.at[f], squares.at[f], sq_s.at[j - 1], sq_r.at[j - 1], ((f + j) % 8, p))

    def cp_sq_from(j):
        return remote(squares.at[f], squares.at[(f + 8 - j) % 8], sq_s.at[j - 1], sq_r.at[j - 1], ((f + j) % 8, p))

    mine, others = pl.ds(HALF * core, HALF), pl.ds(HALF * (1 - core), HALF)

    def w_local():
        return (
            pltpu.make_async_copy(w_gate.at[:, mine], w_in.at[core, :, pl.ds(0, HALF)], w_l.at[0]),
            pltpu.make_async_copy(w_up.at[:, mine], w_in.at[core, :, pl.ds(HALF, HALF)], w_l.at[1]),
            pltpu.make_async_copy(w_down.at[mine, :], w_out.at[core], w_l.at[2]),
        )

    def w_remote(side):
        return (
            remote(w_gate.at[:, others], w_in.at[side, :, pl.ds(0, HALF)], w_s.at[0], w_r.at[0], twin),
            remote(w_up.at[:, others], w_in.at[side, :, pl.ds(HALF, HALF)], w_s.at[1], w_r.at[1], twin),
            remote(w_down.at[others, :], w_out.at[side], w_s.at[2], w_r.at[2], twin),
        )

    def cp_a(i):
        e = expert_of(i)
        return remote(sent.at[e], slots.at[i, core, x, par], a_s.at[i], a_r.at[i], along_z(e))

    def cp_c(i, j):
        own = slots.at[i, core, x, par]
        return remote(own, own, c_s.at[i, j - 1], c_r.at[i, j - 1], same_group(j))

    def cp_d(i, side):
        return remote(slots.at[i, core], slots.at[i, side], d_s.at[i], d_r.at[i], twin)

    def cp_e(i):
        return (
            remote(part.at[i, opp, 0], ra.at[i, 0], e_s.at[i, 0], e_r.at[i, 0], at_y(right)),
            remote(part.at[i, opp, 1], ra.at[i, 1], e_s.at[i, 1], e_r.at[i, 1], at_y(left)),
        )

    def cp_f(i):
        return (
            remote(part.at[i, right], rb.at[i, 0], f_s.at[i, 0], f_r.at[i, 0], at_y(right)),
            remote(part.at[i, left], rb.at[i, 1], f_s.at[i, 1], f_r.at[i, 1], at_y(left)),
        )

    def cp_g(i, to_right, to_left):
        return (
            remote(hid.at[i, y], hid.at[i, to_right], g_s.at[i, 0], g_r.at[i, 0], at_y(right)),
            remote(hid.at[i, y], hid.at[i, to_left], g_s.at[i, 1], g_r.at[i, 1], at_y(left)),
        )

    def cp_h(i, to_right, to_left):
        return (
            remote(hid.at[i, left, 0], hid.at[i, to_right, 0], h_s.at[i, 0], h_r.at[i, 0], at_y(right)),
            remote(hid.at[i, right, 1], hid.at[i, to_left, 1], h_s.at[i, 1], h_r.at[i, 1], at_y(left)),
        )

    def cp_i(i):
        return remote(out_sent.at[i], out_got.at[i], i_s.at[i], i_r.at[i], twin)

    def cp_j(i, j):
        other = (member + j) % 8
        return remote(xs.at[i, other % 4, other // 4], xr.at[i, j - 1], j_s.at[i, j - 1], j_r.at[i, j - 1], same_group(j))

    def cp_l(i):
        return remote(ret_sent.at[i], ret.at[expert], l_s.at[i], l_r.at[i], along_z(source_of(i)))

    def cp_l_from(i):
        return remote(ret_sent.at[i], ret.at[expert_of(i)], l_s.at[i], l_r.at[i], along_z(source_of(i)))

    for copy in w_local():
        copy.start()
    barrier = pltpu.get_barrier_semaphore()
    for j in range(1, 8):
        pl.semaphore_signal(barrier, inc=1, device_id=((f + j) % 8, p), device_id_type=MESH)
        pl.semaphore_signal(barrier, inc=1, device_id=same_group(j), device_id_type=MESH)
        pl.semaphore_signal(barrier, inc=1, device_id=along_z((expert + j) % 8), device_id_type=MESH)

    rows = resid[...].astype(F32)
    squared = rows * rows
    squares[f] = squared[:, 0:128] + squared[:, 128:256] + squared[:, 256:384] + squared[:, 384:512]
    pl.semaphore_wait(barrier, 21)
    for j in range(1, 8):
        cp_sq(j).start()
    for copy in w_remote(core):
        copy.start()

    live = lax.broadcasted_iota(jnp.int32, (LEN, 1), 0) < lengths[p]
    first, second = chosen[:, 0:1], chosen[:, 1:2]
    lanes = lax.broadcasted_iota(jnp.int32, (LEN, 128), 1)
    hits = jnp.where(((lanes == first) | (lanes == second)) & live, 1.0, 0.0)
    before = jnp.where(
        lax.broadcasted_iota(jnp.int32, (LEN, LEN), 1) < lax.broadcasted_iota(jnp.int32, (LEN, LEN), 0), 1.0, 0.0
    )
    rank = jnp.dot(before.astype(BF16), hits.astype(BF16), preferred_element_type=F32)
    places = lax.broadcasted_iota(jnp.int32, (LEN, ROWS), 1).astype(F32)

    def table(pick):
        slot = jnp.sum(jnp.where(lanes == pick, rank, 0.0), axis=1, keepdims=True)
        place = jnp.where(live, pick.astype(F32) * CAP + slot, -1.0)
        return jnp.where(places == place, 1.0, 0.0)

    table_first, table_second = table(first), table(second)
    choose = (table_first + table_second).astype(BF16)

    for j in range(1, 8):
        cp_sq_from(j).wait_recv()
    total = squares[0]
    for j in range(1, 8):
        total = total + squares[j]
    mean = jnp.sum(total, axis=1, keepdims=True) / D
    normed = (rows * lax.rsqrt(mean + 1e-05) * gain[...]).astype(BF16)
    packed = lax.dot_general(choose, normed, (((0,), (0,)), ((), ())), preferred_element_type=F32)
    sent[...] = to_blocks(packed[:, :WIDE], packed[:, WIDE:]).astype(BF16)
    for i in range(1, CHUNKS):
        cp_a(i).start()
    slots[0, core, x, par] = sent[expert]

    def step(t, carry):
        def stage(offset, body):
            i = t - offset

            @pl.when((i >= 0) & (i < CHUNKS))
            def _():
                body(i)

        def gate_up(i):
            @pl.when(i == 0)
            def _():
                for copy in w_local()[:2]:
                    copy.wait()
                for copy in w_remote(1 - core)[:2]:
                    copy.wait_recv()

            cp_d(i, 1 - core).wait_recv()
            halves = []
            for side in range(2):
                block = slots[i, side].reshape(8, BLOCK, WIDE).astype(F32)
                halves.extend(from_blocks(block))
            operand = jnp.concatenate(halves, axis=1).astype(BF16)
            for h in range(2):
                for n in range(HALF // WIDE):
                    columns = pl.ds(h * HALF + n * WIDE, WIDE)
                    product = jnp.dot(operand[:, :FEAT], w_in[0, :, columns], preferred_element_type=F32)
                    product += jnp.dot(operand[:, FEAT:], w_in[1, :, columns], preferred_element_type=F32)
                    part[i, :, h, :, pl.ds(n * WIDE, WIDE)] = product.reshape(4, OWN, WIDE).astype(BF16)
            for copy in cp_e(i):
                copy.start()

        def second_hop(i):
            from_left, from_right = cp_e(i)
            from_left.wait_recv()
            part[i, right, 0] = (part[i, right, 0].astype(F32) + ra[i, 0].astype(F32)).astype(BF16)
            to_right, to_left = cp_f(i)
            to_right.start()
            from_right.wait_recv()
            part[i, left, 1] = (part[i, left, 1].astype(F32) + ra[i, 1].astype(F32)).astype(BF16)
            to_left.start()

        def activate(i):
            for copy in cp_f(i):
                copy.wait_recv()
            gate = part[i, y, 0].astype(F32) + rb[i, 0, 0].astype(F32) + rb[i, 1, 0].astype(F32)
            up = part[i, y, 1].astype(F32) + rb[i, 0, 1].astype(F32) + rb[i, 1, 1].astype(F32)
            value = (gate / (1.0 + jnp.exp(-gate)) * up).astype(BF16)
            hid[i, y, 0] = value[:, : HALF // 2]
            hid[i, y, 1] = value[:, HALF // 2 :]
            for copy in cp_g(i, y, y):
                copy.start()

        def pass_on(i):
            from_left, from_right = cp_g(i, left, right)
            to_right, to_left = cp_h(i, left, right)
            from_left.wait_recv()
            to_right.start()
            from_right.wait_recv()
            to_left.start()

        def down(i):
            @pl.when(i == 0)
            def _():
                w_local()[2].wait()
                w_remote(1 - core)[2].wait_recv()

            for copy in cp_h(i, opp, opp):
                copy.wait_recv()
            operand = jnp.concatenate(
                [hid[i, :, 0].reshape(ROWS, HALF // 2), hid[i, :, 1].reshape(ROWS, HALF // 2)], axis=1
            )

            def product(side):
                return to_blocks(
                    jnp.dot(operand, w_out[side, :, pl.ds(0, WIDE)], preferred_element_type=F32),
                    jnp.dot(operand, w_out[side, :, pl.ds(WIDE, WIDE)], preferred_element_type=F32),
                )

            out_sent[i] = product(1 - core).astype(BF16)
            cp_i(i).start()
            out_mine[i] = product(core)

        def over_slices(i):
            cp_i(i).wait_recv()
            both = out_mine[i] + out_got[i].astype(F32)
            out_mine[i] = both
            xs[i] = both.reshape(4, 2, BLOCK, WIDE).astype(BF16)
            for j in range(1, 8):
                cp_j(i, j).start()

        def give_back(i):
            for j in range(1, 8):
                cp_j(i, j).wait_recv()
            total = out_mine[i, x * 2 + par]
            for j in range(1, 8):
                total = total + xr[i, j - 1].astype(F32)
            ret_sent[i] = total.astype(BF16)

            @pl.when(i == 0)
            def _():
                ret[expert] = ret_sent[i]

            @pl.when(i > 0)
            def _():
                cp_l(i).start()

        def to_twin(i):
            for j in range(1, 8):
                other = (member + 8 - j) % 8
                from_other = slots.at[i, core, other % 4, other // 4]
                remote(from_other, from_other, c_s.at[i, j - 1], c_r.at[i, j - 1], same_group(j)).wait_recv()
            cp_d(i, core).start()

        def to_group(i):
            @pl.when(i > 0)
            def _():
                cp_a(i).wait_recv()

            for j in range(1, 8):
                cp_c(i, j).start()

        stage(2, gate_up)
        stage(3, second_hop)
        stage(4, activate)
        stage(5, pass_on)
        stage(6, down)
        stage(7, over_slices)
        stage(8, give_back)
        stage(1, to_twin)
        stage(0, to_group)
        return carry

    lax.fori_loop(0, CHUNKS + 8, step, 0)

    for i in range(1, CHUNKS):
        cp_l_from(i).wait_recv()
    halves = [half.astype(BF16) for half in from_blocks(ret[...].astype(F32))]
    for h in range(2):
        got_first = jnp.dot(table_first.astype(BF16), halves[h], preferred_element_type=F32)
        got_second = jnp.dot(table_second.astype(BF16), halves[h], preferred_element_type=F32)
        mixed = weight[:, 0:1] * got_first + weight[:, 1:2] * got_second
        out[:, pl.ds(h * WIDE, WIDE)] = mixed.astype(BF16)

    for j in range(1, 8):
        cp_sq(j).wait_send()
    for copy in w_remote(core):
        copy.wait_send()

    def finish(i, carry):
        @pl.when(i > 0)
        def _():
            cp_a(i).wait_send()
            cp_l(i).wait_send()

        for j in range(1, 8):
            cp_c(i, j).wait_send()
            cp_j(i, j).wait_send()
        cp_d(i, core).wait_send()
        cp_i(i).wait_send()
        for copy in (*cp_e(i), *cp_f(i), *cp_g(i, y, y), *cp_h(i, left, right)):
            copy.wait_send()
        return carry

    lax.fori_loop(0, CHUNKS, finish, 0)


def on_device(resid, norm_gain, lengths, route_ids, route_weight, w_gate, w_up, w_down):
    vmem = pl.BlockSpec(memory_space=pltpu.VMEM)
    whole = pl.BlockSpec(memory_space=pl.ANY)
    dma = pltpu.SemaphoreType.DMA
    n = CHUNKS
    result = pl.pallas_call(
        kernel,
        out_shape=jax.ShapeDtypeStruct((LEN, FEAT), BF16),
        in_specs=[pl.BlockSpec(memory_space=pltpu.SMEM), vmem, vmem, vmem, vmem, whole, whole, whole],
        out_specs=vmem,
        scratch_shapes=[
            pltpu.VMEM((8, LEN, 128), F32),
            pltpu.VMEM((EXPERTS, BLOCK, WIDE), BF16),
            pltpu.VMEM((n, 2, 4, 2, BLOCK, WIDE), BF16),
            pltpu.VMEM((2, FEAT, 2 * HALF), BF16),
            pltpu.VMEM((2, HALF, FEAT), BF16),
            pltpu.VMEM((n, 4, 2, OWN, HALF), BF16),
            pltpu.VMEM((n, 2, OWN, HALF), BF16),
            pltpu.VMEM((n, 2, 2, OWN, HALF), BF16),
            pltpu.VMEM((n, 4, 2, OWN, HALF // 2), BF16),
            pltpu.VMEM((n, 8, BLOCK, WIDE), F32),
            pltpu.VMEM((n, 8, BLOCK, WIDE), BF16),
            pltpu.VMEM((n, 8, BLOCK, WIDE), BF16),
            pltpu.VMEM((n, 4, 2, BLOCK, WIDE), BF16),
            pltpu.VMEM((n, 7, BLOCK, WIDE), BF16),
            pltpu.VMEM((n, BLOCK, WIDE), BF16),
            pltpu.VMEM((EXPERTS, BLOCK, WIDE), BF16),
            dma((7,)), dma((7,)),
            dma((3,)), dma((3,)), dma((3,)),
            dma((n,)), dma((n,)),
            dma((n, 7)), dma((n, 7)),
            dma((n,)), dma((n,)),
            dma((n, 2)), dma((n, 2)),
            dma((n, 2)), dma((n, 2)),
            dma((n, 2)), dma((n, 2)),
            dma((n, 2)), dma((n, 2)),
            dma((n,)), dma((n,)),
            dma((n, 7)), dma((n, 7)),
            dma((n,)), dma((n,)),
        ],
        compiler_params=pltpu.CompilerParams(
            collective_id=0, has_side_effects=True, vmem_limit_bytes=52 << 20
        ),
        cost_estimate=pl.CostEstimate(flops=8_000_000_000, bytes_accessed=5_000_000, transcendentals=1_000_000),
    )(lengths, resid[0], norm_gain[None], route_ids[0], route_weight[0], w_gate, w_up, w_down)
    return result[None]


def solution(mesh):
    return jax.shard_map(
        on_device,
        mesh=mesh,
        in_specs=(
            P("expert", None, "fsdp"),
            P("fsdp"),
            P(),
            P("expert", None, None),
            P("expert", None, None),
            P("fsdp", "expert"),
            P("fsdp", "expert"),
            P("expert", "fsdp"),
        ),
        out_specs=P("expert", None, "fsdp"),
        check_vma=False,
    )
```

```python
import jax
import jax.numpy as jnp
from jax import lax
from jax.experimental import pallas as pl
from jax.experimental.pallas import tpu as pltpu
from jax.sharding import PartitionSpec as P

MESH = pl.DeviceIdType.MESH
D = 4096
EXPERTS = 8
CAP = 24
LEN = 64
FEAT = 512
HALF = 768
BLOCK = 2 * CAP
WIDE = 256
CHUNKS = 8
ROWS = 8 * CAP
OWN = ROWS // 4
ORDER = (0, 1, 2, 6, 3, 5, 4, 7)
F32 = jnp.float32
BF16 = jnp.bfloat16


def order_of(i):
    distance = ORDER[0] + 0 * i
    for k in range(1, CHUNKS):
        distance = distance + (ORDER[k] - ORDER[k - 1]) * ((i + CHUNKS - k) // CHUNKS)
    return distance


def to_blocks(left, right):
    return jnp.concatenate([left.reshape(8, CAP, WIDE), right.reshape(8, CAP, WIDE)], axis=1)


def from_blocks(blocks):
    return blocks[:, :CAP, :].reshape(ROWS, WIDE), blocks[:, CAP:, :].reshape(ROWS, WIDE)


def kernel(lengths, resid_in, gain_in, chosen_in, weight_in, w_gate, w_up, w_down, out,
           resid, gain, gain_s, gain_r, chosen, weight, in_l, sq_sent, sq_got, sent, slots, w_in, w_out, part, ra, rb, hid, out_mine, out_sent, out_got,
           xs, xr, ret_sent, ret,
           sq_s, sq_r, w_l, w_s, w_r, a_s, a_r, c_s, c_r, d_s, d_r, e_s, e_r, f_s, f_r, g_s, g_r,
           h_s, h_r, i_s, i_r, j_s, j_r, l_s, l_r):
    f = lax.axis_index("fsdp")
    p = lax.axis_index("expert")
    y, core = f // 2, f % 2
    z, x = p // 4, p % 4
    expert, par = z // 2, z % 2
    member = par * 4 + x
    right, left, opp = (y + 1) % 4, (y + 3) % 4, (y + 2) % 4

    def same_group(j):
        other = (member + j) % 8
        return (f, (2 * expert + other // 4) * 4 + other % 4)

    def along_z(e):
        return (f, (2 * e + par) * 4 + x)

    def at_y(row):
        return (row * 2 + core, p)

    twin = (y * 2 + 1 - core, p)

    def expert_of(i):
        return (expert + CHUNKS - order_of(i)) % CHUNKS

    def source_of(i):
        return (expert + order_of(i)) % CHUNKS

    def remote(src, dst, send, recv, device):
        return pltpu.make_async_remote_copy(
            src_ref=src, dst_ref=dst, send_sem=send, recv_sem=recv, device_id=device, device_id_type=MESH
        )

    def cp_sq(i):
        return (
            remote(sq_sent.at[i, right], sq_got.at[i, 0], sq_s.at[i, 0], sq_r.at[i, 0], at_y(right)),
            remote(sq_sent.at[i, left], sq_got.at[i, 1], sq_s.at[i, 1], sq_r.at[i, 1], at_y(left)),
            remote(sq_sent.at[i, opp], sq_got.at[i, 2], sq_s.at[i, 2], sq_r.at[i, 2], at_y(opp)),
        )

    def cp_gain(side):
        return remote(gain_in, gain.at[side], gain_s, gain_r, twin)

    mine, others = pl.ds(HALF * core, HALF), pl.ds(HALF * (1 - core), HALF)

    def w_local():
        return (
            pltpu.make_async_copy(w_gate.at[:, mine], w_in.at[core, :, pl.ds(0, HALF)], w_l.at[0]),
            pltpu.make_async_copy(w_up.at[:, mine], w_in.at[core, :, pl.ds(HALF, HALF)], w_l.at[1]),
            pltpu.make_async_copy(w_down.at[mine, :], w_out.at[core], w_l.at[2]),
        )

    def w_remote(side):
        return (
            remote(w_gate.at[:, others], w_in.at[side, :, pl.ds(0, HALF)], w_s.at[0], w_r.at[0], twin),
            remote(w_up.at[:, others], w_in.at[side, :, pl.ds(HALF, HALF)], w_s.at[1], w_r.at[1], twin),
            remote(w_down.at[others, :], w_out.at[side], w_s.at[2], w_r.at[2], twin),
        )

    def cp_a(i):
        e = expert_of(i)
        return remote(sent.at[e], slots.at[i, core, x, par], a_s.at[i], a_r.at[i], along_z(e))

    def cp_c(i, j):
        own = slots.at[i, core, x, par]
        return remote(own, own, c_s.at[i, j - 1], c_r.at[i, j - 1], same_group(j))

    def cp_d(i, side):
        return remote(slots.at[i, core], slots.at[i, side], d_s.at[i], d_r.at[i], twin)

    def cp_e(i):
        return (
            remote(part.at[i, opp, 0], ra.at[i, 0], e_s.at[i, 0], e_r.at[i, 0], at_y(right)),
            remote(part.at[i, opp, 1], ra.at[i, 1], e_s.at[i, 1], e_r.at[i, 1], at_y(left)),
        )

    def cp_f(i):
        return (
            remote(part.at[i, right], rb.at[i, 0], f_s.at[i, 0], f_r.at[i, 0], at_y(right)),
            remote(part.at[i, left], rb.at[i, 1], f_s.at[i, 1], f_r.at[i, 1], at_y(left)),
        )

    def cp_g(i, to_right, to_left):
        return (
            remote(hid.at[i, y], hid.at[i, to_right], g_s.at[i, 0], g_r.at[i, 0], at_y(right)),
            remote(hid.at[i, y], hid.at[i, to_left], g_s.at[i, 1], g_r.at[i, 1], at_y(left)),
        )

    def cp_h(i, to_right, to_left):
        return (
            remote(hid.at[i, left, 0], hid.at[i, to_right, 0], h_s.at[i, 0], h_r.at[i, 0], at_y(right)),
            remote(hid.at[i, right, 1], hid.at[i, to_left, 1], h_s.at[i, 1], h_r.at[i, 1], at_y(left)),
        )

    def cp_i(i):
        return remote(out_sent.at[i], out_got.at[i], i_s.at[i], i_r.at[i], twin)

    def cp_j(i, j):
        other = (member + j) % 8
        return remote(xs.at[i, other % 4, other // 4], xr.at[i, j - 1], j_s.at[i, j - 1], j_r.at[i, j - 1], same_group(j))

    def cp_l(i):
        return remote(ret_sent.at[i], ret.at[expert], l_s.at[i], l_r.at[i], along_z(source_of(i)))

    def cp_l_from(i):
        return remote(ret_sent.at[i], ret.at[expert_of(i)], l_s.at[i], l_r.at[i], along_z(source_of(i)))

    small = [
        pltpu.make_async_copy(source, target, in_l.at[k])
        for k, (source, target) in enumerate(
            ((chosen_in, chosen), (resid_in, resid), (weight_in, weight), (gain_in, gain.at[core]))
        )
    ]
    barrier = pltpu.get_barrier_semaphore()
    near = [along_z((expert + 1) % 8), along_z((expert + 7) % 8)]
    near += [same_group(j) for j in range(1, 8)] + [at_y(right), at_y(left), at_y(opp), twin]
    for device in near:
        pl.semaphore_signal(barrier, inc=1, device_id=device, device_id_type=MESH)
    for copy in small:
        copy.start()
    for copy in w_local():
        copy.start()

    def to_column(row, size):
        shape = (size, 128)
        diagonal = lax.broadcasted_iota(jnp.int32, shape, 0) == lax.broadcasted_iota(jnp.int32, shape, 1)
        return jnp.sum(jnp.where(diagonal, row, 0.0), axis=1, keepdims=True)

    small[0].wait()
    live = lax.broadcasted_iota(jnp.int32, (1, LEN), 1) < lengths[p]
    first, second = chosen[0:1, :], chosen[1:2, :]
    experts = lax.broadcasted_iota(jnp.int32, (EXPERTS, LEN), 0)
    hits = jnp.where(((experts == first) | (experts == second)) & live, 1.0, 0.0)
    before = jnp.where(
        lax.broadcasted_iota(jnp.int32, (LEN, LEN), 0) < lax.broadcasted_iota(jnp.int32, (LEN, LEN), 1), 1.0, 0.0
    )
    rank = jnp.dot(hits.astype(BF16), before.astype(BF16), preferred_element_type=F32)
    places = lax.broadcasted_iota(jnp.int32, (ROWS, LEN), 0).astype(F32)

    def table(pick):
        slot = jnp.sum(jnp.where(experts == pick, rank, 0.0), axis=0, keepdims=True)
        place = jnp.where(live, pick.astype(F32) * CAP + slot, -1.0)
        return jnp.where(places == place, 1.0, 0.0)

    table_first, table_second = table(first), table(second)
    choose = (table_first + table_second).astype(BF16)

    def weight_of(k):
        row = jnp.concatenate([weight[k : k + 1, :], jnp.zeros((1, 128 - LEN), F32)], axis=1)
        return to_column(row, LEN)

    small[1].wait()
    packed = jnp.dot(choose, resid[...], preferred_element_type=F32)
    sent[...] = to_blocks(packed[:, :WIDE], packed[:, WIDE:]).astype(BF16)
    slots[0, core, x, par] = sent[expert]
    pl.semaphore_wait(barrier, len(near))
    for j in range(1, 8):
        cp_c(0, j).start()
    cp_a(1).start()
    cp_a(7).start()
    cp_gain(core).start()
    for copy in w_remote(core):
        copy.start()
    for copy in small[2:]:
        copy.wait()

    def step(t, carry):
        def stage(offset, body, begin=0):
            i = t - offset

            @pl.when((i >= begin) & (i < CHUNKS))
            def _():
                body(i)

        def gate_up(i):
            @pl.when(i == 0)
            def _():
                cp_gain(1 - core).wait_recv()
                for copy in w_local()[:2]:
                    copy.wait()
                for copy in w_remote(1 - core)[:2]:
                    copy.wait_recv()

            cp_d(i, 1 - core).wait_recv()
            halves = []
            for side in range(2):
                block = slots[i, side].reshape(8, BLOCK, WIDE).astype(F32)
                halves.extend(from_blocks(block))
            squared = halves[0] * halves[0]
            for half in halves[1:]:
                squared += half * half
            column = jnp.sum(squared, axis=1, keepdims=True).reshape(4, OWN, 1)
            shape = (4, OWN, 128)
            diagonal = lax.broadcasted_iota(jnp.int32, shape, 1) == lax.broadcasted_iota(jnp.int32, shape, 2)
            row = jnp.sum(jnp.where(diagonal, column, 0.0), axis=1, keepdims=True)
            sq_sent[i] = jnp.broadcast_to(row, (4, 8, 128))
            for copy in cp_sq(i):
                copy.start()
            gained = [halves[k] * gain[k // 2, :, pl.ds(k % 2 * WIDE, WIDE)] for k in range(4)]
            operand = jnp.concatenate(gained, axis=1).astype(BF16)
            for h in range(2):
                for n in range(HALF // WIDE):
                    columns = pl.ds(h * HALF + n * WIDE, WIDE)
                    product = jnp.dot(operand[:, :FEAT], w_in[0, :, columns], preferred_element_type=F32)
                    product += jnp.dot(operand[:, FEAT:], w_in[1, :, columns], preferred_element_type=F32)
                    part[i, :, h, :, pl.ds(n * WIDE, WIDE)] = product.reshape(4, OWN, WIDE).astype(BF16)
            for copy in cp_e(i):
                copy.start()

        def second_hop(i):
            from_left, from_right = cp_e(i)
            from_left.wait_recv()
            part[i, right, 0] = (part[i, right, 0].astype(F32) + ra[i, 0].astype(F32)).astype(BF16)
            to_right, to_left = cp_f(i)
            to_right.start()
            from_right.wait_recv()
            part[i, left, 1] = (part[i, left, 1].astype(F32) + ra[i, 1].astype(F32)).astype(BF16)
            to_left.start()

        def activate(i):
            for copy in (*cp_f(i), *cp_sq(i)):
                copy.wait_recv()
            total = sq_sent[i, y] + sq_got[i, 0] + sq_got[i, 1] + sq_got[i, 2]
            scale = lax.rsqrt(to_column(total[0:1, :], OWN) / D + 1e-05)
            gate = part[i, y, 0].astype(F32) + rb[i, 0, 0].astype(F32) + rb[i, 1, 0].astype(F32)
            up = part[i, y, 1].astype(F32) + rb[i, 0, 1].astype(F32) + rb[i, 1, 1].astype(F32)
            gate, up = gate * scale, up * scale
            value = (gate / (1.0 + jnp.exp(-gate)) * up).astype(BF16)
            hid[i, y, 0] = value[:, : HALF // 2]
            hid[i, y, 1] = value[:, HALF // 2 :]
            for copy in cp_g(i, y, y):
                copy.start()

        def pass_on(i):
            from_left, from_right = cp_g(i, left, right)
            to_right, to_left = cp_h(i, left, right)
            from_left.wait_recv()
            to_right.start()
            from_right.wait_recv()
            to_left.start()

        def down(i):
            @pl.when(i == 0)
            def _():
                w_local()[2].wait()
                w_remote(1 - core)[2].wait_recv()

            for copy in cp_h(i, opp, opp):
                copy.wait_recv()
            operand = jnp.concatenate(
                [hid[i, :, 0].reshape(ROWS, HALF // 2), hid[i, :, 1].reshape(ROWS, HALF // 2)], axis=1
            )

            def product(side):
                return to_blocks(
                    jnp.dot(operand, w_out[side, :, pl.ds(0, WIDE)], preferred_element_type=F32),
                    jnp.dot(operand, w_out[side, :, pl.ds(WIDE, WIDE)], preferred_element_type=F32),
                )

            out_sent[i] = product(1 - core).astype(BF16)
            cp_i(i).start()
            out_mine[i] = product(core)

        def over_slices(i):
            cp_i(i).wait_recv()
            both = out_mine[i] + out_got[i].astype(F32)
            out_mine[i] = both
            xs[i] = both.reshape(4, 2, BLOCK, WIDE).astype(BF16)
            for j in range(1, 8):
                cp_j(i, j).start()

        def give_back(i):
            for j in range(1, 8):
                cp_j(i, j).wait_recv()
            total = out_mine[i, x * 2 + par]
            for j in range(1, 8):
                total = total + xr[i, j - 1].astype(F32)
            ret_sent[i] = total.astype(BF16)

            @pl.when(i == 0)
            def _():
                ret[expert] = ret_sent[i]

            @pl.when(i > 0)
            def _():
                cp_l(i).start()

        def to_twin(i):
            for j in range(1, 8):
                other = (member + 8 - j) % 8
                from_other = slots.at[i, core, other % 4, other // 4]
                remote(from_other, from_other, c_s.at[i, j - 1], c_r.at[i, j - 1], same_group(j)).wait_recv()
            cp_d(i, core).start()

        def to_group(i):
            for j in range(1, 8):
                cp_c(i, j).start()

        for at, arrived, leaving in ((1, (1, 7), (2, 3)), (2, (2, 3), (4, 5)), (4, (4, 5), (6,)), (6, (6,), ())):

            @pl.when(t == at)
            def _(arrived=arrived, leaving=leaving):
                for i in arrived:
                    cp_a(i).wait_recv()
                for i in leaving:
                    cp_a(i).start()

        stage(0, to_group, 1)
        stage(2, gate_up)
        stage(3, second_hop)
        stage(1, to_twin)
        stage(4, activate)
        stage(5, pass_on)
        stage(6, down)
        stage(7, over_slices)
        stage(9, give_back)
        return carry

    lax.fori_loop(0, CHUNKS + 9, step, 0)

    for i in range(1, CHUNKS):
        cp_l_from(i).wait_recv()
    halves = [half.astype(BF16) for half in from_blocks(ret[...].astype(F32))]
    over_slots = (((0,), (0,)), ((), ()))
    for h in range(2):
        got_first = lax.dot_general(table_first.astype(BF16), halves[h], over_slots, preferred_element_type=F32)
        got_second = lax.dot_general(table_second.astype(BF16), halves[h], over_slots, preferred_element_type=F32)
        mixed = weight_of(0) * got_first + weight_of(1) * got_second
        out[:, pl.ds(h * WIDE, WIDE)] = mixed.astype(BF16)

    for copy in (cp_gain(core), *w_remote(core)):
        copy.wait_send()

    def finish(i, carry):
        @pl.when(i > 0)
        def _():
            cp_a(i).wait_send()
            cp_l(i).wait_send()

        for j in range(1, 8):
            cp_c(i, j).wait_send()
            cp_j(i, j).wait_send()
        cp_d(i, core).wait_send()
        cp_i(i).wait_send()
        for copy in (*cp_sq(i), *cp_e(i), *cp_f(i), *cp_g(i, y, y), *cp_h(i, left, right)):
            copy.wait_send()
        return carry

    lax.fori_loop(0, CHUNKS, finish, 0)


def on_device(resid, norm_gain, lengths, route_ids, route_weight, w_gate, w_up, w_down):
    vmem = pl.BlockSpec(memory_space=pltpu.VMEM)
    whole = pl.BlockSpec(memory_space=pl.ANY)
    dma = pltpu.SemaphoreType.DMA
    n = CHUNKS
    result = pl.pallas_call(
        kernel,
        out_shape=jax.ShapeDtypeStruct((LEN, FEAT), BF16),
        in_specs=[pl.BlockSpec(memory_space=pltpu.SMEM)] + [whole] * 7,
        out_specs=vmem,
        scratch_shapes=[
            pltpu.VMEM((LEN, FEAT), BF16),
            pltpu.VMEM((2, 1, FEAT), F32),
            dma, dma,
            pltpu.VMEM((2, LEN), jnp.int32),
            pltpu.VMEM((2, LEN), F32),
            dma((4,)),
            pltpu.VMEM((n, 4, 8, 128), F32),
            pltpu.VMEM((n, 3, 8, 128), F32),
            pltpu.VMEM((EXPERTS, BLOCK, WIDE), BF16),
            pltpu.VMEM((n, 2, 4, 2, BLOCK, WIDE), BF16),
            pltpu.VMEM((2, FEAT, 2 * HALF), BF16),
            pltpu.VMEM((2, HALF, FEAT), BF16),
            pltpu.VMEM((n, 4, 2, OWN, HALF), BF16),
            pltpu.VMEM((n, 2, OWN, HALF), BF16),
            pltpu.VMEM((n, 2, 2, OWN, HALF), BF16),
            pltpu.VMEM((n, 4, 2, OWN, HALF // 2), BF16),
            pltpu.VMEM((n, 8, BLOCK, WIDE), F32),
            pltpu.VMEM((n, 8, BLOCK, WIDE), BF16),
            pltpu.VMEM((n, 8, BLOCK, WIDE), BF16),
            pltpu.VMEM((n, 4, 2, BLOCK, WIDE), BF16),
            pltpu.VMEM((n, 7, BLOCK, WIDE), BF16),
            pltpu.VMEM((n, BLOCK, WIDE), BF16),
            pltpu.VMEM((EXPERTS, BLOCK, WIDE), BF16),
            dma((n, 3)), dma((n, 3)),
            dma((3,)), dma((3,)), dma((3,)),
            dma((n,)), dma((n,)),
            dma((n, 7)), dma((n, 7)),
            dma((n,)), dma((n,)),
            dma((n, 2)), dma((n, 2)),
            dma((n, 2)), dma((n, 2)),
            dma((n, 2)), dma((n, 2)),
            dma((n, 2)), dma((n, 2)),
            dma((n,)), dma((n,)),
            dma((n, 7)), dma((n, 7)),
            dma((n,)), dma((n,)),
        ],
        compiler_params=pltpu.CompilerParams(
            collective_id=0, has_side_effects=True, vmem_limit_bytes=60 << 20
        ),
        cost_estimate=pl.CostEstimate(flops=8_000_000_000, bytes_accessed=5_000_000, transcendentals=1_000_000),
    )(lengths, resid[0], norm_gain[None], route_ids[0].T, route_weight[0].T, w_gate, w_up, w_down)
    return result[None]


def solution(mesh):
    return jax.shard_map(
        on_device,
        mesh=mesh,
        in_specs=(
            P("expert", None, "fsdp"),
            P("fsdp"),
            P(),
            P("expert", None, None),
            P("expert", None, None),
            P("fsdp", "expert"),
            P("fsdp", "expert"),
            P("expert", "fsdp"),
        ),
        out_specs=P("expert", None, "fsdp"),
        check_vma=False,
    )
```

```python
import jax
import jax.numpy as jnp
from jax import lax
from jax.experimental import pallas as pl
from jax.experimental.pallas import tpu as pltpu
from jax.sharding import PartitionSpec as P

MESH = pl.DeviceIdType.MESH
D = 4096
EXPERTS = 8
CAP = 24
LEN = 64
FEAT = 512
HALF = 768
BLOCK = 2 * CAP
WIDE = 256
CHUNKS = 8
ROWS = 8 * CAP
OWN = ROWS // 4
ORDER = (0, 1, 2, 6, 3, 5, 4, 7)
F32 = jnp.float32
BF16 = jnp.bfloat16


def order_of(i):
    distance = ORDER[0] + 0 * i
    for k in range(1, CHUNKS):
        distance = distance + (ORDER[k] - ORDER[k - 1]) * ((i + CHUNKS - k) // CHUNKS)
    return distance


def to_blocks(left, right):
    return jnp.concatenate([left.reshape(8, CAP, WIDE), right.reshape(8, CAP, WIDE)], axis=1)


def from_blocks(blocks):
    return blocks[:, :CAP, :].reshape(ROWS, WIDE), blocks[:, CAP:, :].reshape(ROWS, WIDE)


def kernel(lengths, resid_in, gain_in, chosen_in, weight_in, w_gate, w_up, w_down, out,
           resid, gain, gain_s, gain_r, chosen, weight, tables, shares, in_l, sq_sent, sq_got, sent, slots, w_in, w_out, part, ra, rb, hid, out_mine, out_sent, out_got,
           xs, xr, ret_sent, ret,
           sq_s, sq_r, w_l, w_s, w_r, a_s, a_r, c_s, c_r, d_s, d_r, e_s, e_r, f_s, f_r, g_s, g_r,
           h_s, h_r, i_s, i_r, j_s, j_r, l_s, l_r):
    f = lax.axis_index("fsdp")
    p = lax.axis_index("expert")
    y, core = f // 2, f % 2
    z, x = p // 4, p % 4
    expert, par = z // 2, z % 2
    member = par * 4 + x
    right, left, opp = (y + 1) % 4, (y + 3) % 4, (y + 2) % 4

    def same_group(j):
        other = (member + j) % 8
        return (f, (2 * expert + other // 4) * 4 + other % 4)

    def along_z(e):
        return (f, (2 * e + par) * 4 + x)

    def at_y(row):
        return (row * 2 + core, p)

    twin = (y * 2 + 1 - core, p)

    def expert_of(i):
        return (expert + CHUNKS - order_of(i)) % CHUNKS

    def source_of(i):
        return (expert + order_of(i)) % CHUNKS

    def remote(src, dst, send, recv, device):
        return pltpu.make_async_remote_copy(
            src_ref=src, dst_ref=dst, send_sem=send, recv_sem=recv, device_id=device, device_id_type=MESH
        )

    def cp_sq(i):
        return (
            remote(sq_sent.at[i, right], sq_got.at[i, 0], sq_s.at[i, 0], sq_r.at[i, 0], at_y(right)),
            remote(sq_sent.at[i, left], sq_got.at[i, 1], sq_s.at[i, 1], sq_r.at[i, 1], at_y(left)),
            remote(sq_sent.at[i, opp], sq_got.at[i, 2], sq_s.at[i, 2], sq_r.at[i, 2], at_y(opp)),
        )

    def cp_gain(side):
        return remote(gain_in, gain.at[side], gain_s, gain_r, twin)

    mine, others = pl.ds(HALF * core, HALF), pl.ds(HALF * (1 - core), HALF)

    def w_local():
        return (
            pltpu.make_async_copy(w_gate.at[:, mine], w_in.at[core, :, pl.ds(0, HALF)], w_l.at[0]),
            pltpu.make_async_copy(w_up.at[:, mine], w_in.at[core, :, pl.ds(HALF, HALF)], w_l.at[1]),
            pltpu.make_async_copy(w_down.at[mine, :], w_out.at[core], w_l.at[2]),
        )

    def w_remote(side):
        return (
            remote(w_gate.at[:, others], w_in.at[side, :, pl.ds(0, HALF)], w_s.at[0], w_r.at[0], twin),
            remote(w_up.at[:, others], w_in.at[side, :, pl.ds(HALF, HALF)], w_s.at[1], w_r.at[1], twin),
            remote(w_down.at[others, :], w_out.at[side], w_s.at[2], w_r.at[2], twin),
        )

    def cp_a(i):
        e = expert_of(i)
        return remote(sent.at[e], slots.at[i, core, x, par], a_s.at[i], a_r.at[i], along_z(e))

    def cp_c(i, j):
        own = slots.at[i, core, x, par]
        return remote(own, own, c_s.at[i, j - 1], c_r.at[i, j - 1], same_group(j))

    def cp_d(i, side):
        return remote(slots.at[i, core], slots.at[i, side], d_s.at[i], d_r.at[i], twin)

    def cp_e(i):
        return (
            remote(part.at[i, opp, 0], ra.at[i, 0], e_s.at[i, 0], e_r.at[i, 0], at_y(right)),
            remote(part.at[i, opp, 1], ra.at[i, 1], e_s.at[i, 1], e_r.at[i, 1], at_y(left)),
        )

    def cp_f(i):
        return (
            remote(part.at[i, right], rb.at[i, 0], f_s.at[i, 0], f_r.at[i, 0], at_y(right)),
            remote(part.at[i, left], rb.at[i, 1], f_s.at[i, 1], f_r.at[i, 1], at_y(left)),
        )

    def cp_g(i, to_right, to_left):
        return (
            remote(hid.at[i, y], hid.at[i, to_right], g_s.at[i, 0], g_r.at[i, 0], at_y(right)),
            remote(hid.at[i, y], hid.at[i, to_left], g_s.at[i, 1], g_r.at[i, 1], at_y(left)),
        )

    def cp_h(i, to_right, to_left):
        return (
            remote(hid.at[i, left, 0], hid.at[i, to_right, 0], h_s.at[i, 0], h_r.at[i, 0], at_y(right)),
            remote(hid.at[i, right, 1], hid.at[i, to_left, 1], h_s.at[i, 1], h_r.at[i, 1], at_y(left)),
        )

    def cp_i(i):
        return remote(out_sent.at[i], out_got.at[i], i_s.at[i], i_r.at[i], twin)

    def cp_j(i, j):
        other = (member + j) % 8
        return remote(xs.at[i, other % 4, other // 4], xr.at[i, j - 1], j_s.at[i, j - 1], j_r.at[i, j - 1], same_group(j))

    def cp_l(i):
        return remote(ret_sent.at[i], ret.at[expert], l_s.at[i], l_r.at[i], along_z(source_of(i)))

    def cp_l_from(i):
        return remote(ret_sent.at[i], ret.at[expert_of(i)], l_s.at[i], l_r.at[i], along_z(source_of(i)))

    small = [
        pltpu.make_async_copy(source, target, in_l.at[k])
        for k, (source, target) in enumerate(
            ((chosen_in, chosen), (resid_in, resid), (weight_in, weight), (gain_in, gain.at[core]))
        )
    ]
    barrier = pltpu.get_barrier_semaphore()
    near = [along_z((expert + 1) % 8), along_z((expert + 7) % 8)]
    near += [same_group(j) for j in range(1, 8)] + [at_y(right), at_y(left), at_y(opp), twin]
    for device in near:
        pl.semaphore_signal(barrier, inc=1, device_id=device, device_id_type=MESH)
    for copy in small:
        copy.start()
    for copy in w_local():
        copy.start()

    def to_column(row, size):
        shape = (size, 128)
        diagonal = lax.broadcasted_iota(jnp.int32, shape, 0) == lax.broadcasted_iota(jnp.int32, shape, 1)
        return jnp.sum(jnp.where(diagonal, row, 0.0), axis=1, keepdims=True)

    small[0].wait()
    live = lax.broadcasted_iota(jnp.int32, (1, LEN), 1) < lengths[p]
    first, second = chosen[0:1, :], chosen[1:2, :]
    experts = lax.broadcasted_iota(jnp.int32, (EXPERTS, LEN), 0)
    hits = jnp.where(((experts == first) | (experts == second)) & live, 1.0, 0.0)
    before = jnp.where(
        lax.broadcasted_iota(jnp.int32, (LEN, LEN), 0) < lax.broadcasted_iota(jnp.int32, (LEN, LEN), 1), 1.0, 0.0
    )
    rank = jnp.dot(hits.astype(BF16), before.astype(BF16), preferred_element_type=F32)
    places = lax.broadcasted_iota(jnp.int32, (ROWS, LEN), 0).astype(F32)

    def wide(row):
        return jnp.concatenate([row, jnp.zeros((1, 128 - LEN), F32)], axis=1)

    def place_for(pick):
        slot = jnp.sum(jnp.where(experts == pick, rank, 0.0), axis=0, keepdims=True)
        return jnp.where(live, pick.astype(F32) * CAP + slot, -1.0)

    chosen_places = (place_for(first), place_for(second))
    choose = sum(jnp.where(places == place, 1.0, 0.0) for place in chosen_places).astype(BF16)

    small[1].wait()
    packed = jnp.dot(choose, resid[...], preferred_element_type=F32)
    sent[...] = to_blocks(packed[:, :WIDE], packed[:, WIDE:]).astype(BF16)
    slots[0, core, x, par] = sent[expert]
    pl.semaphore_wait(barrier, len(near))
    for j in range(1, 8):
        cp_c(0, j).start()
    cp_a(1).start()
    cp_a(7).start()
    cp_gain(core).start()
    for copy in w_remote(core):
        copy.start()
    for copy in small[2:]:
        copy.wait()

    lanes = lax.broadcasted_iota(jnp.int32, (LEN, ROWS), 1).astype(F32)
    for k in range(2):
        tables[k] = jnp.where(lanes == to_column(wide(chosen_places[k]), LEN), 1.0, 0.0).astype(BF16)
        shares[k] = jnp.broadcast_to(to_column(wide(weight[k : k + 1, :]), LEN), (LEN, WIDE))

    def step(t, carry):
        def stage(offset, body, begin=0):
            i = t - offset

            @pl.when((i >= begin) & (i < CHUNKS))
            def _():
                body(i)

        def gate_up(i):
            @pl.when(i == 0)
            def _():
                cp_gain(1 - core).wait_recv()
                for copy in w_local()[:2]:
                    copy.wait()
                for copy in w_remote(1 - core)[:2]:
                    copy.wait_recv()

            cp_d(i, 1 - core).wait_recv()
            halves = []
            for side in range(2):
                block = slots[i, side].reshape(8, BLOCK, WIDE).astype(F32)
                halves.extend(from_blocks(block))
            gained = [halves[k] * gain[k // 2, :, pl.ds(k % 2 * WIDE, WIDE)] for k in range(4)]
            operand = jnp.concatenate(gained, axis=1).astype(BF16)
            for h in range(2):
                for n in range(HALF // WIDE):
                    columns = pl.ds(h * HALF + n * WIDE, WIDE)
                    product = jnp.dot(operand[:, :FEAT], w_in[0, :, columns], preferred_element_type=F32)
                    product += jnp.dot(operand[:, FEAT:], w_in[1, :, columns], preferred_element_type=F32)
                    part[i, :, h, :, pl.ds(n * WIDE, WIDE)] = product.reshape(4, OWN, WIDE).astype(BF16)
                cp_e(i)[h].start()
            squared = halves[0] * halves[0]
            for half in halves[1:]:
                squared += half * half
            column = jnp.sum(squared, axis=1, keepdims=True).reshape(4, OWN, 1)
            shape = (4, OWN, 128)
            diagonal = lax.broadcasted_iota(jnp.int32, shape, 1) == lax.broadcasted_iota(jnp.int32, shape, 2)
            row = jnp.sum(jnp.where(diagonal, column, 0.0), axis=1, keepdims=True)
            sq_sent[i] = jnp.broadcast_to(row, (4, 8, 128))
            for copy in cp_sq(i):
                copy.start()

        def second_hop(i):
            from_left, from_right = cp_e(i)
            from_left.wait_recv()
            part[i, right, 0] = (part[i, right, 0].astype(F32) + ra[i, 0].astype(F32)).astype(BF16)
            to_right, to_left = cp_f(i)
            to_right.start()
            from_right.wait_recv()
            part[i, left, 1] = (part[i, left, 1].astype(F32) + ra[i, 1].astype(F32)).astype(BF16)
            to_left.start()

        def activate(i):
            for copy in (*cp_f(i), *cp_sq(i)):
                copy.wait_recv()
            total = sq_sent[i, y] + sq_got[i, 0] + sq_got[i, 1] + sq_got[i, 2]
            scale = lax.rsqrt(to_column(total[0:1, :], OWN) / D + 1e-05)
            gate = part[i, y, 0].astype(F32) + rb[i, 0, 0].astype(F32) + rb[i, 1, 0].astype(F32)
            up = part[i, y, 1].astype(F32) + rb[i, 0, 1].astype(F32) + rb[i, 1, 1].astype(F32)
            gate, up = gate * scale, up * scale
            value = (gate / (1.0 + jnp.exp(-gate)) * up).astype(BF16)
            hid[i, y, 0] = value[:, : HALF // 2]
            hid[i, y, 1] = value[:, HALF // 2 :]
            for copy in cp_g(i, y, y):
                copy.start()

        def pass_on(i):
            from_left, from_right = cp_g(i, left, right)
            to_right, to_left = cp_h(i, left, right)
            from_left.wait_recv()
            to_right.start()
            from_right.wait_recv()
            to_left.start()

        def down(i):
            @pl.when(i == 0)
            def _():
                w_local()[2].wait()
                w_remote(1 - core)[2].wait_recv()

            for copy in cp_h(i, opp, opp):
                copy.wait_recv()
            operand = jnp.concatenate(
                [hid[i, :, 0].reshape(ROWS, HALF // 2), hid[i, :, 1].reshape(ROWS, HALF // 2)], axis=1
            )

            def product(side):
                return to_blocks(
                    jnp.dot(operand, w_out[side, :, pl.ds(0, WIDE)], preferred_element_type=F32),
                    jnp.dot(operand, w_out[side, :, pl.ds(WIDE, WIDE)], preferred_element_type=F32),
                )

            out_sent[i] = product(1 - core).astype(BF16)
            cp_i(i).start()
            out_mine[i] = product(core)

        def over_slices(i):
            cp_i(i).wait_recv()
            both = out_mine[i] + out_got[i].astype(F32)
            out_mine[i] = both
            xs[i] = both.reshape(4, 2, BLOCK, WIDE).astype(BF16)
            for j in range(1, 8):
                cp_j(i, j).start()

        def give_back(i):
            for j in range(1, 8):
                cp_j(i, j).wait_recv()
            total = out_mine[i, x * 2 + par]
            for j in range(1, 8):
                total = total + xr[i, j - 1].astype(F32)
            ret_sent[i] = total.astype(BF16)

            @pl.when(i == 0)
            def _():
                ret[expert] = ret_sent[i]

            @pl.when(i > 0)
            def _():
                cp_l(i).start()

        def finish(i):
            @pl.when(i == 0)
            def _():
                for copy in (cp_gain(core), *w_remote(core)):
                    copy.wait_send()

            @pl.when(i > 0)
            def _():
                cp_a(i).wait_send()

            for j in range(1, 8):
                cp_c(i, j).wait_send()
                cp_j(i, j).wait_send()
            cp_d(i, core).wait_send()
            cp_i(i).wait_send()
            for copy in (*cp_sq(i), *cp_e(i), *cp_f(i), *cp_g(i, y, y), *cp_h(i, left, right)):
                copy.wait_send()

        def to_twin(i):
            for j in range(1, 8):
                other = (member + 8 - j) % 8
                from_other = slots.at[i, core, other % 4, other // 4]
                remote(from_other, from_other, c_s.at[i, j - 1], c_r.at[i, j - 1], same_group(j)).wait_recv()
            cp_d(i, core).start()

        def to_group(i):
            for j in range(1, 8):
                cp_c(i, j).start()

        stage(3, second_hop)
        stage(2, gate_up)
        stage(1, to_twin)
        stage(4, activate)
        for at, arrived, leaving in ((1, (1, 7), (2, 3)), (2, (2, 3), (4, 5)), (4, (4, 5), (6,)), (6, (6,), ())):

            @pl.when(t == at)
            def _(arrived=arrived, leaving=leaving):
                for i in arrived:
                    cp_a(i).wait_recv()
                for i in leaving:
                    cp_a(i).start()

        stage(0, to_group, 1)
        stage(5, pass_on)
        stage(6, down)
        stage(7, over_slices)
        stage(9, give_back)
        stage(9, finish)
        return carry

    lax.fori_loop(0, CHUNKS + 9, step, 0)

    for i in range(1, CHUNKS):
        cp_l_from(i).wait_recv()
    halves = [half.astype(BF16) for half in from_blocks(ret[...].astype(F32))]
    for h in range(2):
        got = [jnp.dot(tables[k], halves[h], preferred_element_type=F32) for k in range(2)]
        out[:, pl.ds(h * WIDE, WIDE)] = (shares[0] * got[0] + shares[1] * got[1]).astype(BF16)

    for i in range(1, CHUNKS):
        cp_l(i).wait_send()


def on_device(resid, norm_gain, lengths, route_ids, route_weight, w_gate, w_up, w_down):
    vmem = pl.BlockSpec(memory_space=pltpu.VMEM)
    whole = pl.BlockSpec(memory_space=pl.ANY)
    dma = pltpu.SemaphoreType.DMA
    n = CHUNKS
    result = pl.pallas_call(
        kernel,
        out_shape=jax.ShapeDtypeStruct((LEN, FEAT), BF16),
        in_specs=[pl.BlockSpec(memory_space=pltpu.SMEM)] + [whole] * 7,
        out_specs=vmem,
        scratch_shapes=[
            pltpu.VMEM((LEN, FEAT), BF16),
            pltpu.VMEM((2, 1, FEAT), F32),
            dma, dma,
            pltpu.VMEM((2, LEN), jnp.int32),
            pltpu.VMEM((2, LEN), F32),
            pltpu.VMEM((2, LEN, ROWS), BF16),
            pltpu.VMEM((2, LEN, WIDE), F32),
            dma((4,)),
            pltpu.VMEM((n, 4, 8, 128), F32),
            pltpu.VMEM((n, 3, 8, 128), F32),
            pltpu.VMEM((EXPERTS, BLOCK, WIDE), BF16),
            pltpu.VMEM((n, 2, 4, 2, BLOCK, WIDE), BF16),
            pltpu.VMEM((2, FEAT, 2 * HALF), BF16),
            pltpu.VMEM((2, HALF, FEAT), BF16),
            pltpu.VMEM((n, 4, 2, OWN, HALF), BF16),
            pltpu.VMEM((n, 2, OWN, HALF), BF16),
            pltpu.VMEM((n, 2, 2, OWN, HALF), BF16),
            pltpu.VMEM((n, 4, 2, OWN, HALF // 2), BF16),
            pltpu.VMEM((n, 8, BLOCK, WIDE), F32),
            pltpu.VMEM((n, 8, BLOCK, WIDE), BF16),
            pltpu.VMEM((n, 8, BLOCK, WIDE), BF16),
            pltpu.VMEM((n, 4, 2, BLOCK, WIDE), BF16),
            pltpu.VMEM((n, 7, BLOCK, WIDE), BF16),
            pltpu.VMEM((n, BLOCK, WIDE), BF16),
            pltpu.VMEM((EXPERTS, BLOCK, WIDE), BF16),
            dma((n, 3)), dma((n, 3)),
            dma((3,)), dma((3,)), dma((3,)),
            dma((n,)), dma((n,)),
            dma((n, 7)), dma((n, 7)),
            dma((n,)), dma((n,)),
            dma((n, 2)), dma((n, 2)),
            dma((n, 2)), dma((n, 2)),
            dma((n, 2)), dma((n, 2)),
            dma((n, 2)), dma((n, 2)),
            dma((n,)), dma((n,)),
            dma((n, 7)), dma((n, 7)),
            dma((n,)), dma((n,)),
        ],
        compiler_params=pltpu.CompilerParams(
            collective_id=0, has_side_effects=True, vmem_limit_bytes=60 << 20
        ),
        cost_estimate=pl.CostEstimate(flops=8_000_000_000, bytes_accessed=5_000_000, transcendentals=1_000_000),
    )(lengths, resid[0], norm_gain[None], route_ids[0].T, route_weight[0].T, w_gate, w_up, w_down)
    return result[None]


def solution(mesh):
    return jax.shard_map(
        on_device,
        mesh=mesh,
        in_specs=(
            P("expert", None, "fsdp"),
            P("fsdp"),
            P(),
            P("expert", None, None),
            P("expert", None, None),
            P("fsdp", "expert"),
            P("fsdp", "expert"),
            P("expert", "fsdp"),
        ),
        out_specs=P("expert", None, "fsdp"),
        check_vma=False,
    )
```

```python
import jax
import jax.numpy as jnp
from jax import lax
from jax.experimental import pallas as pl
from jax.experimental.pallas import tpu as pltpu
from jax.sharding import PartitionSpec as P

MESH = pl.DeviceIdType.MESH
D = 4096
EXPERTS = 8
CAP = 24
LEN = 64
FEAT = 512
HALF = 768
BLOCK = 2 * CAP
WIDE = 256
CHUNKS = 8
ROWS = 8 * CAP
OWN = ROWS // 4
ORDER = (0, 1, 2, 6, 3, 5, 4, 7)
F32 = jnp.float32
BF16 = jnp.bfloat16


def order_of(i):
    distance = ORDER[0] + 0 * i
    for k in range(1, CHUNKS):
        distance = distance + (ORDER[k] - ORDER[k - 1]) * ((i + CHUNKS - k) // CHUNKS)
    return distance


def to_blocks(left, right):
    return jnp.concatenate([left.reshape(8, CAP, WIDE), right.reshape(8, CAP, WIDE)], axis=1)


def from_blocks(blocks):
    return blocks[:, :CAP, :].reshape(ROWS, WIDE), blocks[:, CAP:, :].reshape(ROWS, WIDE)


def kernel(lengths, resid_in, gain_in, chosen_in, weight_in, w_gate, w_up, w_down, out,
           resid, gain, gain_s, gain_r, chosen, weight, tables, shares, in_l, sq_sent, sq_got, sent, slots, w_in, w_out, part, ra, rb, hid, out_mine, out_sent, out_got,
           xs, xr, ret_sent, ret,
           sq_s, sq_r, w_l, w_s, w_r, a_s, a_r, c_s, c_r, d_s, d_r, e_s, e_r, f_s, f_r, g_s, g_r,
           h_s, h_r, i_s, i_r, j_s, j_r, l_s, l_r):
    f = lax.axis_index("fsdp")
    p = lax.axis_index("expert")
    y, core = f // 2, f % 2
    z, x = p // 4, p % 4
    expert, par = z // 2, z % 2
    member = par * 4 + x
    right, left, opp = (y + 1) % 4, (y + 3) % 4, (y + 2) % 4

    def same_group(j):
        other = (member + j) % 8
        return (f, (2 * expert + other // 4) * 4 + other % 4)

    def along_z(e):
        return (f, (2 * e + par) * 4 + x)

    def at_y(row):
        return (row * 2 + core, p)

    twin = (y * 2 + 1 - core, p)

    def expert_of(i):
        return (expert + CHUNKS - order_of(i)) % CHUNKS

    def source_of(i):
        return (expert + order_of(i)) % CHUNKS

    def remote(src, dst, send, recv, device):
        return pltpu.make_async_remote_copy(
            src_ref=src, dst_ref=dst, send_sem=send, recv_sem=recv, device_id=device, device_id_type=MESH
        )

    def cp_sq(i):
        return (
            remote(sq_sent.at[i, right], sq_got.at[i, 0], sq_s.at[i, 0], sq_r.at[i, 0], at_y(right)),
            remote(sq_sent.at[i, left], sq_got.at[i, 1], sq_s.at[i, 1], sq_r.at[i, 1], at_y(left)),
            remote(sq_sent.at[i, opp], sq_got.at[i, 2], sq_s.at[i, 2], sq_r.at[i, 2], at_y(opp)),
        )

    def cp_gain(side):
        return remote(gain_in, gain.at[side], gain_s, gain_r, twin)

    mine, others = pl.ds(HALF * core, HALF), pl.ds(HALF * (1 - core), HALF)

    def w_local():
        return (
            pltpu.make_async_copy(w_gate.at[:, mine], w_in.at[core, :, pl.ds(0, HALF)], w_l.at[0]),
            pltpu.make_async_copy(w_up.at[:, mine], w_in.at[core, :, pl.ds(HALF, HALF)], w_l.at[1]),
            pltpu.make_async_copy(w_down.at[mine, :], w_out.at[core], w_l.at[2]),
        )

    def w_remote(side):
        return (
            remote(w_gate.at[:, others], w_in.at[side, :, pl.ds(0, HALF)], w_s.at[0], w_r.at[0], twin),
            remote(w_up.at[:, others], w_in.at[side, :, pl.ds(HALF, HALF)], w_s.at[1], w_r.at[1], twin),
            remote(w_down.at[others, :], w_out.at[side], w_s.at[2], w_r.at[2], twin),
        )

    def cp_a(i):
        e = expert_of(i)
        return remote(sent.at[e], slots.at[i, core, x, par], a_s.at[i], a_r.at[i], along_z(e))

    def cp_c(i, j):
        own = slots.at[i, core, x, par]
        return remote(own, own, c_s.at[i, j - 1], c_r.at[i, j - 1], same_group(j))

    def cp_d(i, side):
        return remote(slots.at[i, core], slots.at[i, side], d_s.at[i], d_r.at[i], twin)

    def cp_e(i):
        return (
            remote(part.at[i, opp, 0], ra.at[i, 0], e_s.at[i, 0], e_r.at[i, 0], at_y(right)),
            remote(part.at[i, opp, 1], ra.at[i, 1], e_s.at[i, 1], e_r.at[i, 1], at_y(left)),
        )

    def cp_f(i):
        return (
            remote(part.at[i, right], rb.at[i, 0], f_s.at[i, 0], f_r.at[i, 0], at_y(right)),
            remote(part.at[i, left], rb.at[i, 1], f_s.at[i, 1], f_r.at[i, 1], at_y(left)),
        )

    def cp_g(i, to_right, to_left):
        return (
            remote(hid.at[i, y], hid.at[i, to_right], g_s.at[i, 0], g_r.at[i, 0], at_y(right)),
            remote(hid.at[i, y], hid.at[i, to_left], g_s.at[i, 1], g_r.at[i, 1], at_y(left)),
        )

    def cp_h(i, to_right, to_left):
        return (
            remote(hid.at[i, left, 0], hid.at[i, to_right, 0], h_s.at[i, 0], h_r.at[i, 0], at_y(right)),
            remote(hid.at[i, right, 1], hid.at[i, to_left, 1], h_s.at[i, 1], h_r.at[i, 1], at_y(left)),
        )

    def cp_i(i):
        return remote(out_sent.at[i], out_got.at[i], i_s.at[i], i_r.at[i], twin)

    def cp_j(i, j):
        other = (member + j) % 8
        return remote(xs.at[i, other % 4, other // 4], xr.at[i, j - 1], j_s.at[i, j - 1], j_r.at[i, j - 1], same_group(j))

    def cp_l(i):
        return remote(ret_sent.at[i], ret.at[expert], l_s.at[i], l_r.at[i], along_z(source_of(i)))

    def cp_l_from(i):
        return remote(ret_sent.at[i], ret.at[expert_of(i)], l_s.at[i], l_r.at[i], along_z(source_of(i)))

    small = [
        pltpu.make_async_copy(source, target, in_l.at[k])
        for k, (source, target) in enumerate(
            ((chosen_in, chosen), (resid_in, resid), (weight_in, weight), (gain_in, gain.at[core]))
        )
    ]
    barrier = pltpu.get_barrier_semaphore()
    near = [along_z((expert + 1) % 8), along_z((expert + 7) % 8)]
    near += [same_group(j) for j in range(1, 8)] + [at_y(right), at_y(left), at_y(opp), twin]
    for device in near:
        pl.semaphore_signal(barrier, inc=1, device_id=device, device_id_type=MESH)
    for copy in small:
        copy.start()
    for copy in w_local():
        copy.start()

    def to_column(row, size):
        shape = (size, 128)
        diagonal = lax.broadcasted_iota(jnp.int32, shape, 0) == lax.broadcasted_iota(jnp.int32, shape, 1)
        return jnp.sum(jnp.where(diagonal, row, 0.0), axis=1, keepdims=True)

    small[0].wait()
    live = lax.broadcasted_iota(jnp.int32, (1, LEN), 1) < lengths[p]
    first, second = chosen[0:1, :], chosen[1:2, :]
    experts = lax.broadcasted_iota(jnp.int32, (EXPERTS, LEN), 0)
    hits = jnp.where(((experts == first) | (experts == second)) & live, 1.0, 0.0)
    before = jnp.where(
        lax.broadcasted_iota(jnp.int32, (LEN, LEN), 0) < lax.broadcasted_iota(jnp.int32, (LEN, LEN), 1), 1.0, 0.0
    )
    rank = jnp.dot(hits.astype(BF16), before.astype(BF16), preferred_element_type=F32)
    places = lax.broadcasted_iota(jnp.int32, (ROWS, LEN), 0).astype(F32)

    def wide(row):
        return jnp.concatenate([row, jnp.zeros((1, 128 - LEN), F32)], axis=1)

    def place_for(pick):
        slot = jnp.sum(jnp.where(experts == pick, rank, 0.0), axis=0, keepdims=True)
        return jnp.where(live, pick.astype(F32) * CAP + slot, -1.0)

    chosen_places = (place_for(first), place_for(second))
    choose = sum(jnp.where(places == place, 1.0, 0.0) for place in chosen_places).astype(BF16)

    small[1].wait()
    packed = jnp.dot(choose, resid[...], preferred_element_type=F32)
    sent[...] = to_blocks(packed[:, :WIDE], packed[:, WIDE:]).astype(BF16)
    slots[0, core, x, par] = sent[expert]
    pl.semaphore_wait(barrier, len(near))
    for j in range(1, 8):
        cp_c(0, j).start()
    cp_a(1).start()
    cp_a(7).start()
    cp_gain(core).start()
    for copy in w_remote(core)[:2]:
        copy.start()
    for copy in small[2:]:
        copy.wait()

    lanes = lax.broadcasted_iota(jnp.int32, (LEN, ROWS), 1).astype(F32)
    for k in range(2):
        tables[k] = jnp.where(lanes == to_column(wide(chosen_places[k]), LEN), 1.0, 0.0).astype(BF16)
        shares[k] = jnp.broadcast_to(to_column(wide(weight[k : k + 1, :]), LEN), (LEN, WIDE))

    def step(t, carry):
        def stage(offset, body, begin=0, end=CHUNKS):
            i = t - offset

            @pl.when((i >= begin) & (i < end))
            def _():
                body(i)

        def gate_up(i):
            @pl.when(i == 0)
            def _():
                cp_gain(1 - core).wait_recv()
                w_local()[0].wait()
                w_remote(1 - core)[0].wait_recv()

            cp_d(i, 1 - core).wait_recv()
            halves = []
            for side in range(2):
                block = slots[i, side].reshape(8, BLOCK, WIDE).astype(F32)
                halves.extend(from_blocks(block))
            gained = [halves[k] * gain[k // 2, :, pl.ds(k % 2 * WIDE, WIDE)] for k in range(4)]
            operand = jnp.concatenate(gained, axis=1).astype(BF16)
            for h in range(2):
                if h == 1:

                    @pl.when(i == 0)
                    def _():
                        w_local()[1].wait()
                        w_remote(1 - core)[1].wait_recv()
                        w_remote(core)[2].start()

                for n in range(HALF // WIDE):
                    columns = pl.ds(h * HALF + n * WIDE, WIDE)
                    product = jnp.dot(operand[:, :FEAT], w_in[0, :, columns], preferred_element_type=F32)
                    product += jnp.dot(operand[:, FEAT:], w_in[1, :, columns], preferred_element_type=F32)
                    part[i, :, h, :, pl.ds(n * WIDE, WIDE)] = product.reshape(4, OWN, WIDE).astype(BF16)
                cp_e(i)[h].start()
            squared = halves[0] * halves[0]
            for half in halves[1:]:
                squared += half * half
            column = jnp.sum(squared, axis=1, keepdims=True).reshape(4, OWN, 1)
            shape = (4, OWN, 128)
            diagonal = lax.broadcasted_iota(jnp.int32, shape, 1) == lax.broadcasted_iota(jnp.int32, shape, 2)
            row = jnp.sum(jnp.where(diagonal, column, 0.0), axis=1, keepdims=True)
            sq_sent[i] = jnp.broadcast_to(row, (4, 8, 128))
            for copy in cp_sq(i):
                copy.start()

        def second_hop(i):
            from_left, from_right = cp_e(i)
            from_left.wait_recv()
            part[i, right, 0] = (part[i, right, 0].astype(F32) + ra[i, 0].astype(F32)).astype(BF16)
            to_right, to_left = cp_f(i)
            to_right.start()
            from_right.wait_recv()
            part[i, left, 1] = (part[i, left, 1].astype(F32) + ra[i, 1].astype(F32)).astype(BF16)
            to_left.start()

        def activate(i):
            for copy in (*cp_f(i), *cp_sq(i)):
                copy.wait_recv()
            total = sq_sent[i, y] + sq_got[i, 0] + sq_got[i, 1] + sq_got[i, 2]
            scale = lax.rsqrt(to_column(total[0:1, :], OWN) / D + 1e-05)
            gate = part[i, y, 0].astype(F32) + rb[i, 0, 0].astype(F32) + rb[i, 1, 0].astype(F32)
            up = part[i, y, 1].astype(F32) + rb[i, 0, 1].astype(F32) + rb[i, 1, 1].astype(F32)
            gate, up = gate * scale, up * scale
            value = (gate / (1.0 + jnp.exp(-gate)) * up).astype(BF16)
            hid[i, y, 0] = value[:, : HALF // 2]
            hid[i, y, 1] = value[:, HALF // 2 :]
            for copy in cp_g(i, y, y):
                copy.start()

        def pass_on(i):
            from_left, from_right = cp_g(i, left, right)
            to_right, to_left = cp_h(i, left, right)
            from_left.wait_recv()
            to_right.start()
            from_right.wait_recv()
            to_left.start()

        def down(i):
            @pl.when(i == 0)
            def _():
                w_local()[2].wait()
                w_remote(1 - core)[2].wait_recv()

            for copy in cp_h(i, opp, opp):
                copy.wait_recv()
            operand = jnp.concatenate(
                [hid[i, :, 0].reshape(ROWS, HALF // 2), hid[i, :, 1].reshape(ROWS, HALF // 2)], axis=1
            )

            def product(side):
                return to_blocks(
                    jnp.dot(operand, w_out[side, :, pl.ds(0, WIDE)], preferred_element_type=F32),
                    jnp.dot(operand, w_out[side, :, pl.ds(WIDE, WIDE)], preferred_element_type=F32),
                )

            out_sent[i] = product(1 - core).astype(BF16)
            cp_i(i).start()
            out_mine[i] = product(core)

        def over_slices(i):
            cp_i(i).wait_recv()
            both = out_mine[i] + out_got[i].astype(F32)
            out_mine[i] = both
            xs[i] = both.reshape(4, 2, BLOCK, WIDE).astype(BF16)
            for j in range(1, 8):
                cp_j(i, j).start()

        def give_back(i):
            for j in range(1, 8):
                cp_j(i, j).wait_recv()
            total = out_mine[i, x * 2 + par]
            for j in range(1, 8):
                total = total + xr[i, j - 1].astype(F32)
            ret_sent[i] = total.astype(BF16)

            @pl.when(i == 0)
            def _():
                ret[expert] = ret_sent[i]

            @pl.when(i > 0)
            def _():
                cp_l(i).start()

        def finish(i):
            @pl.when(i == 0)
            def _():
                for copy in (cp_gain(core), *w_remote(core)):
                    copy.wait_send()

            @pl.when(i > 0)
            def _():
                cp_a(i).wait_send()

            for j in range(1, 8):
                cp_c(i, j).wait_send()
                cp_j(i, j).wait_send()
            cp_d(i, core).wait_send()
            cp_i(i).wait_send()
            for copy in (*cp_sq(i), *cp_e(i), *cp_f(i), *cp_g(i, y, y), *cp_h(i, left, right)):
                copy.wait_send()

        def to_twin(i):
            for j in range(1, 8):
                other = (member + 8 - j) % 8
                from_other = slots.at[i, core, other % 4, other // 4]
                remote(from_other, from_other, c_s.at[i, j - 1], c_r.at[i, j - 1], same_group(j)).wait_recv()
            cp_d(i, core).start()

        def to_group(i):
            for j in range(1, 8):
                cp_c(i, j).start()

        stage(3, second_hop)
        stage(2, gate_up)
        stage(1, to_twin)
        stage(4, activate)
        for at, arrived, leaving in ((1, (1, 7), (2, 3)), (2, (2, 3), (4, 5)), (3, (4, 5), (6,)), (5, (6,), ())):

            @pl.when(t == at)
            def _(arrived=arrived, leaving=leaving):
                for i in arrived:
                    cp_a(i).wait_recv()
                for i in leaving:
                    cp_a(i).start()

        stage(0, to_group, 1, 3)
        stage(-1, to_group, 3)
        stage(5, pass_on)
        stage(6, down)
        stage(7, over_slices)
        stage(8, give_back)
        stage(8, finish)
        return carry

    lax.fori_loop(0, CHUNKS + 8, step, 0)

    for i in range(1, CHUNKS):
        cp_l_from(i).wait_recv()
    halves = [half.astype(BF16) for half in from_blocks(ret[...].astype(F32))]
    for h in range(2):
        got = [jnp.dot(tables[k], halves[h], preferred_element_type=F32) for k in range(2)]
        out[:, pl.ds(h * WIDE, WIDE)] = (shares[0] * got[0] + shares[1] * got[1]).astype(BF16)

    for i in range(1, CHUNKS):
        cp_l(i).wait_send()


def on_device(resid, norm_gain, lengths, route_ids, route_weight, w_gate, w_up, w_down):
    vmem = pl.BlockSpec(memory_space=pltpu.VMEM)
    whole = pl.BlockSpec(memory_space=pl.ANY)
    dma = pltpu.SemaphoreType.DMA
    n = CHUNKS
    result = pl.pallas_call(
        kernel,
        out_shape=jax.ShapeDtypeStruct((LEN, FEAT), BF16),
        in_specs=[pl.BlockSpec(memory_space=pltpu.SMEM)] + [whole] * 7,
        out_specs=vmem,
        scratch_shapes=[
            pltpu.VMEM((LEN, FEAT), BF16),
            pltpu.VMEM((2, 1, FEAT), F32),
            dma, dma,
            pltpu.VMEM((2, LEN), jnp.int32),
            pltpu.VMEM((2, LEN), F32),
            pltpu.VMEM((2, LEN, ROWS), BF16),
            pltpu.VMEM((2, LEN, WIDE), F32),
            dma((4,)),
            pltpu.VMEM((n, 4, 8, 128), F32),
            pltpu.VMEM((n, 3, 8, 128), F32),
            pltpu.VMEM((EXPERTS, BLOCK, WIDE), BF16),
            pltpu.VMEM((n, 2, 4, 2, BLOCK, WIDE), BF16),
            pltpu.VMEM((2, FEAT, 2 * HALF), BF16),
            pltpu.VMEM((2, HALF, FEAT), BF16),
            pltpu.VMEM((n, 4, 2, OWN, HALF), BF16),
            pltpu.VMEM((n, 2, OWN, HALF), BF16),
            pltpu.VMEM((n, 2, 2, OWN, HALF), BF16),
            pltpu.VMEM((n, 4, 2, OWN, HALF // 2), BF16),
            pltpu.VMEM((n, 8, BLOCK, WIDE), F32),
            pltpu.VMEM((n, 8, BLOCK, WIDE), BF16),
            pltpu.VMEM((n, 8, BLOCK, WIDE), BF16),
            pltpu.VMEM((n, 4, 2, BLOCK, WIDE), BF16),
            pltpu.VMEM((n, 7, BLOCK, WIDE), BF16),
            pltpu.VMEM((n, BLOCK, WIDE), BF16),
            pltpu.VMEM((EXPERTS, BLOCK, WIDE), BF16),
            dma((n, 3)), dma((n, 3)),
            dma((3,)), dma((3,)), dma((3,)),
            dma((n,)), dma((n,)),
            dma((n, 7)), dma((n, 7)),
            dma((n,)), dma((n,)),
            dma((n, 2)), dma((n, 2)),
            dma((n, 2)), dma((n, 2)),
            dma((n, 2)), dma((n, 2)),
            dma((n, 2)), dma((n, 2)),
            dma((n,)), dma((n,)),
            dma((n, 7)), dma((n, 7)),
            dma((n,)), dma((n,)),
        ],
        compiler_params=pltpu.CompilerParams(
            collective_id=0, has_side_effects=True, vmem_limit_bytes=60 << 20
        ),
        cost_estimate=pl.CostEstimate(flops=8_000_000_000, bytes_accessed=5_000_000, transcendentals=1_000_000),
    )(lengths, resid[0], norm_gain[None], route_ids[0].T, route_weight[0].T, w_gate, w_up, w_down)
    return result[None]


def solution(mesh):
    return jax.shard_map(
        on_device,
        mesh=mesh,
        in_specs=(
            P("expert", None, "fsdp"),
            P("fsdp"),
            P(),
            P("expert", None, None),
            P("expert", None, None),
            P("fsdp", "expert"),
            P("fsdp", "expert"),
            P("expert", "fsdp"),
        ),
        out_specs=P("expert", None, "fsdp"),
        check_vma=False,
    )
```
